512 devices in a mesh: group: 64 (over y_hi, x, z), loop: 8 (over y_lo, core).
Axes of the slice: x: 4, y: 8 (y_hi: 2, y_lo: 4; y = y_hi * 4 + y_lo), z: 8, core: 2. Of those that a mesh axis runs over, the one named last changes fastest.
Arguments:
- queries: float32 [131072, 1024], P(('loop', 'group')), may hold values from -2 to 2
- keys: float32 [131072, 1024], P(('loop', 'group')), may hold values from -1 to 1
- pattern: int32 [512, 5], P(('loop', 'group')), may hold values from 0 to 1, as said below
- positive: int32 [131072], P(('loop', 'group')), may hold values from 0 to 1279, as said below
Outputs:
- loss: float32 [131072], P(('loop', 'group'))
- grad_queries: float32 [131072, 1024], P(('loop', 'group'))
- grad_keys: float32 [131072, 1024], P(('loop', 'group'))
The draws below stay inside these ranges and needn't reach their ends.
Inputs may be any that keep to these rules, and one draw needn't show every extreme that they name: `pattern`: 0 or 1; column 0 is always 1; column 3 is 0 for tiles of band 0 and column 4 is 0 for tiles of band 64 - 1. The neighbour column positive // 256 of the query's tile is allowed by pattern.
All inputs are finite; a program needn't handle non-finite values.
Results may differ from the reference program's by a relative error of at most 0.00045.
Values sent between devices are 32-bit elements; how exact they have to be, the bound alone decides.
No kernel may reach another device: no remote copies, remote signals or barrier semaphores. Data moves between devices by JAX's collectives and lax.ppermute only.
A program may use at most 64 MiB of HBM per device.

```python
import math
import jax
import jax.numpy as jnp
from jax import lax

D = 1024
BLOCK = 256
NEIGH = 5
SECTORS = 8
BANDS = 64
TILES = 512
ROWS = 131072


def embedding_noise(key):
    key = jax.random.fold_in(key, 21)
    return jnp.clip(jax.random.normal(key, (ROWS, D), jnp.float32), -5.0, 5.0) * D ** (-0.5)


def tile_pattern(key):
    key = jax.random.fold_in(key, 31)
    first, second = jax.random.split(key)
    density = jax.random.randint(first, (TILES, 1), 0, 5)
    levels = jax.random.randint(second, (TILES, NEIGH), 0, 4)
    allowed = (levels < density).astype(jnp.int32)
    tile_ids = jnp.arange(TILES, dtype=jnp.int32)[:, None]
    band = tile_ids % BANDS
    column = jnp.arange(NEIGH, dtype=jnp.int32)[None, :]
    allowed = jnp.where(column == 0, 1, allowed)
    allowed = jnp.where((column == 4) & (tile_ids == 0), 1, allowed)
    allowed = jnp.where((column == 3) & (band == 0), 0, allowed)
    allowed = jnp.where((column == 4) & (band == BANDS - 1), 0, allowed)
    return allowed.astype(jnp.int32)


def draw_pattern(key, part):
    allowed = tile_pattern(key)
    return allowed


def draw_positive(key, part):
    allowed = tile_pattern(key)
    key = jax.random.fold_in(key, 5)
    first, second = jax.random.split(key)
    offset = jax.random.randint(first, (ROWS,), 0, NEIGH)
    tile = jnp.arange(ROWS, dtype=jnp.int32) // BLOCK
    usable = allowed[tile, offset]
    offset = jnp.where(usable == 1, offset, 0)
    row = jax.random.randint(second, (ROWS,), 0, BLOCK)
    chosen = (offset * BLOCK + row).astype(jnp.int32)
    index = jnp.arange(ROWS, dtype=jnp.int32)
    chosen = jnp.where(index == BLOCK - 1, NEIGH * BLOCK - 1, chosen)
    chosen = jnp.where(index == 0, 0, chosen)
    return chosen.astype(jnp.int32)


def draw_keys(key, part):
    noise = embedding_noise(key)
    return noise


def draw_queries(key, part):
    key = jax.random.fold_in(key, 9)
    return jnp.clip(jax.random.normal(key, (ROWS, D), jnp.float32), -5.0, 5.0) * D ** (-0.5)


def setup_inputs(seed: int = 0) -> dict:
    seeds = jax.random.split(jax.random.key(seed), 5)
    return {
        "queries": draw_queries(jax.random.fold_in(seeds[4], 71), 0),
        "keys": draw_keys(jax.random.fold_in(seeds[4], 71), 0),
        "pattern": draw_pattern(jax.random.fold_in(seeds[4], 71), 0),
        "positive": draw_positive(jax.random.fold_in(seeds[4], 71), 0),
    }


HIGH = lax.Precision.HIGHEST
SECTOR_STEP = (0, -1, 1, 0, 0)
BAND_STEP = (0, 0, 0, -1, 1)
REVERSE_SLOT = (0, 2, 1, 4, 3)

def neighbour_tiles(tile):
    sector = tile // BANDS
    band = tile % BANDS
    listed = [(sector + step_s) % SECTORS * BANDS + (band + step_b) % BANDS for step_s, step_b in zip(SECTOR_STEP, BAND_STEP)]
    return jnp.stack(listed).astype(jnp.int32)

def reference(queries, keys, pattern, positive):
    sharpness = math.sqrt(D)
    query_tiles = queries.reshape(TILES, BLOCK, D)
    key_tiles = keys.reshape(TILES, BLOCK, D)
    positive_tiles = positive.reshape(TILES, BLOCK)
    slot_ids = jnp.arange(NEIGH * BLOCK, dtype=jnp.int32)
    row_ids = jnp.arange(BLOCK, dtype=jnp.int32)

    def forward(tile):
        near = neighbour_tiles(tile)
        stacked = key_tiles[near]
        rows = query_tiles[tile]
        allowed = pattern[tile] > 0
        mask = allowed[None, :, None]
        scores = jnp.einsum('id,ojd->ioj', rows, stacked, precision=HIGH) * sharpness
        masked = jnp.where(mask, scores, -jnp.inf)
        highest = lax.optimization_barrier(jnp.max(masked, axis=(1, 2)))
        partition = lax.optimization_barrier(jnp.sum(jnp.where(mask, jnp.exp(masked - highest[:, None, None]), 0.0), axis=(1, 2)))
        log_total = highest + jnp.log(partition)
        is_positive = (slot_ids[None, :] == positive_tiles[tile][:, None]).reshape(BLOCK, NEIGH, BLOCK)
        positive_score = lax.optimization_barrier(jnp.sum(jnp.where(is_positive, scores, 0.0), axis=(1, 2)))
        probs = jnp.where(mask, jnp.exp(masked - log_total[:, None, None]), 0.0)
        weights = probs - is_positive.astype(probs.dtype)
        grad_rows = jnp.einsum('ioj,ojd->id', weights, stacked, precision=HIGH) * sharpness
        return (log_total - positive_score, log_total, grad_rows)
    losses, log_totals, grad_q = lax.map(forward, jnp.arange(TILES, dtype=jnp.int32))

    def backward(tile):
        near = neighbour_tiles(tile)
        keys_here = key_tiles[tile]
        summed = jnp.zeros((BLOCK, D), jnp.float32)
        for offset in range(NEIGH):
            source = near[offset]
            back_slot = REVERSE_SLOT[offset]
            rows = query_tiles[source]
            allowed = pattern[source, back_slot] > 0
            scores = jnp.einsum('id,jd->ij', rows, keys_here, precision=HIGH) * sharpness
            probs = jnp.where(allowed, jnp.exp(scores - log_totals[source][:, None]), 0.0)
            is_positive = positive_tiles[source][:, None] == back_slot * BLOCK + row_ids[None, :]
            weights = probs - is_positive.astype(probs.dtype)
            summed = summed + jnp.einsum('ij,id->jd', weights, rows, precision=HIGH) * sharpness
        return summed
    grad_k = lax.map(backward, jnp.arange(TILES, dtype=jnp.int32))
    return (losses.reshape(ROWS), grad_q.reshape(ROWS, D), grad_k.reshape(ROWS, D))
```

```python
import functools
import math

import jax
import jax.numpy as jnp
from jax import lax
from jax.experimental import pallas as pl
from jax.experimental.pallas import tpu as pltpu
from jax.sharding import PartitionSpec as P

FULL = lax.Precision.HIGHEST
AXES = ("group", "loop")
BANDS, SECTORS, ZS = 64, 8, 8
SEAM = 31
FAR = 1e30
VMEM_BYTES = 40 * 1024 * 1024


def at(x, y, z, core):
    band = (y // 4) * 32 + x * ZS + z
    return band * SECTORS + (y % 4) * 2 + core


def seam_column(y, core, which):
    if (y % 4 >= 2) == (which == 1):
        return (3, 0) if core else (0, 7)
    if y < 4:
        return (2, 0) if core else (1, 0)
    return (1, 7) if core else (2, 7)


def seam_pairs(which):
    out, onward = [], []
    for y in range(8):
        for core in range(2):
            up = y < 4
            here = at(3, y, 7, core) if up else at(0, y, 0, core)
            there = at(0, y + 4, 0, core) if up else at(3, y - 4, 7, core)
            x, z = seam_column(y, core, which)
            relay = at(x, y, z, core)
            out.append((here, relay))
            onward.append((relay, there))
    return out, onward


def sector_swap(first):
    pairs = []
    for b in range(BANDS):
        for s in range(first, SECTORS + first, 2):
            i, j = b * SECTORS + s, b * SECTORS + (s + 1) % SECTORS
            pairs += [(i, j), (j, i)]
    return pairs


def band_pairs(b):
    pairs = []
    for s in range(SECTORS):
        i, j = b * SECTORS + s, (b + 1) * SECTORS + s
        pairs += [(i, j), (j, i)]
    return pairs


def band_swap(first):
    return sum([band_pairs(b) for b in range(first, BANDS - 1, 2) if b != SEAM], [])


def seam_swap():
    return band_pairs(SEAM)


def send(value, pairs):
    return lax.ppermute(value, AXES, pairs)


def outer(a, b):
    return lax.dot_general(a, b, (((1,), (1,)), ((), ())), precision=FULL, preferred_element_type=jnp.float32)


def inner(a, b):
    return jnp.dot(a, b, precision=FULL, preferred_element_type=jnp.float32)


def call(body, out, args, smem=0, later=(), flops=0, name=None):
    vmem = pl.BlockSpec(memory_space=pltpu.VMEM)
    scalar = pl.BlockSpec(memory_space=pltpu.SMEM)
    out = [a if isinstance(a, jax.ShapeDtypeStruct) else jax.ShapeDtypeStruct(a, jnp.float32) for a in out]
    moved = sum(a.dtype.itemsize * math.prod(a.shape) for a in list(args) + out)
    count = len(args) - smem
    args = list(args) + list(later)

    def run(*refs):
        body(*refs[:smem + count], *refs[len(args):])

    return pl.pallas_call(
        run,
        out_shape=out,
        in_specs=[scalar] * smem + [vmem] * count + [pl.BlockSpec(memory_space=pl.ANY)] * len(later),
        out_specs=[vmem] * len(out),
        compiler_params=pltpu.CompilerParams(vmem_limit_bytes=VMEM_BYTES),
        cost_estimate=pl.CostEstimate(flops=flops, bytes_accessed=moved, transcendentals=0),
        name=name,
    )(*args)


def mark(out):
    out[...] = jnp.zeros_like(out)


def after(*arrays):
    return call(mark, [(8, 128)], [], later=arrays, name="after")[0]


def passed(value, out):
    out[...] = value[...]


def first_scores(sharpness, q, k, ka, s0, sa):
    big = q[...] * sharpness
    s0[...] = outer(big, k[...])
    sa[...] = outer(big, ka[...])


def scores(sharpness, q, k, s):
    s[...] = outer(q[...] * sharpness, k[...])


def column(row):
    return jnp.broadcast_to(row, (128, row.shape[1])).T[:, :1]


def as_row(col):
    return jnp.broadcast_to(col, (col.shape[0], 128)).T[:1]


def softmax(sharpness, place, allowed, s0, sa, sb, sc, sd, seam, q, positive, weights, loss, aux, term_a, term_b):
    t = q.shape[0]
    for o, s in enumerate((s0, sa, sb, sc, sd)):
        weights[:, o * t:(o + 1) * t] = s[...]

    @pl.when(place[0] > 0)
    def _():
        weights[:, 4 * t:] = outer(q[...] * sharpness, seam[...])

    pick = column(positive[...])
    columns = lax.broadcasted_iota(jnp.int32, (t, t), 1)
    blocks = [weights[:, o * t:(o + 1) * t] for o in range(5)]
    masked = [jnp.where(allowed[place[1 + o]] > 0, b, -FAR) for o, b in enumerate(blocks)]
    highest = jnp.max(functools.reduce(jnp.maximum, masked), axis=1, keepdims=True)
    powers = [jnp.exp(m - highest) for m in masked]
    total = jnp.sum(sum(powers), axis=1, keepdims=True)
    log_total = highest + jnp.log(total)
    hits = [pick == columns + place[1 + o] * t for o in range(5)]
    score = sum(jnp.where(h, b, 0.0) for h, b in zip(hits, blocks))
    loss[...] = as_row(log_total - jnp.sum(score, axis=1, keepdims=True))
    share = sharpness / total
    for o, (p, h) in enumerate(zip(powers, hits)):
        weights[:, o * t:(o + 1) * t] = p * share - jnp.where(h, sharpness, 0.0)
    logs = as_row(log_total)
    aux[...] = jnp.zeros_like(aux)
    aux[0:1] = jnp.where(allowed[place[5]] > 0, logs, FAR)
    aux[1:2] = (positive[...] - place[5] * t).astype(jnp.float32)
    term_a[...] = inner(weights[:, t:2 * t].T, q[...])
    term_b[...] = inner(weights[:, 2 * t:3 * t].T, q[...])


def band_terms(weights, q, term_c, term_d):
    t = q.shape[0]
    term_c[...] = inner(weights[:, 3 * t:4 * t].T, q[...])
    term_d[...] = inner(weights[:, 4 * t:].T, q[...])


def query_gradient(place, weights, q, k, ka, kb, kc, kd, seam, gq, own):
    t = k.shape[0]
    own[...] = inner(weights[:, :t].T, q[...])
    weight = lambda o: weights[:, o * t:(o + 1) * t]
    total = inner(weight(0), k[...])
    for o, key in enumerate((ka, kb, kc)):
        total += inner(weight(o + 1), key[...])
    gq[...] = total

    @pl.when(place[0] > 0)
    def _():
        gq[...] += inner(weight(4), seam[...])

    @pl.when(place[0] == 0)
    def _():
        gq[...] += inner(weight(4), kd[...])


def key_sum(own, ta, tb, tc, td, out):
    out[...] = own[...] + ta[...] + tb[...] + tc[...] + td[...]


def seam_scores(sharpness, place, k, q, s):
    @pl.when(place[0] > 0)
    def _():
        s[...] = outer(k[...] * sharpness, q[...])


def key_gradient(sharpness, place, some, s, q, aux, gk):
    t = s.shape[0]
    gk[...] = some[...]

    @pl.when(place[0] > 0)
    def _():
        rows = lax.broadcasted_iota(jnp.int32, (t, t), 0)
        hits = rows == aux[1:2].astype(jnp.int32)
        w = (jnp.exp(s[...] - aux[0:1]) - jnp.where(hits, 1.0, 0.0)) * sharpness
        gk[...] += inner(w, q[...])


def local(queries, keys, pattern, positive):
    t, d = queries.shape
    sharpness = math.sqrt(d)
    one = 2 * t * t * d
    band, sector = lax.axis_index("group"), lax.axis_index("loop")
    odd_band, odd_sector = band % 2, sector % 2
    at_seam = (band == SEAM) | (band == SEAM + 1)
    place = jnp.stack([
        at_seam.astype(jnp.int32),
        0 * band,
        2 - odd_sector,
        1 + odd_sector,
        4 - odd_band,
        3 + odd_band,
    ])
    swap_a, swap_b = sector_swap(0), sector_swap(1)
    swap_c, swap_d = band_swap(0), band_swap(1)
    out_k, onward_k = seam_pairs(0)
    out_q, onward_q = seam_pairs(1)
    score = functools.partial(call, functools.partial(scores, sharpness), [(t, t)], flops=one)

    hop = send(keys, out_k)
    kb = send(keys, swap_b)
    kc = send(keys, swap_c)
    kd = send(keys, swap_d)
    ka = send(keys, swap_a)
    s0, sa = call(
        functools.partial(first_scores, sharpness),
        [(t, t), (t, t)],
        [queries, keys, ka], later=[hop], flops=2 * one, name="first_scores",
    )
    seam = send(hop, onward_k)
    hop_q = send(queries, out_q)
    (sb,) = score([queries, kb], later=[s0], name="scores_b")
    (sc,) = score([queries, kc], later=[sb], name="scores_c")
    (sd,) = score([queries, kd], later=[sc], name="scores_d")
    seam_q = send(hop_q, onward_q)
    weights, loss, aux, term_a, term_b = call(
        functools.partial(softmax, sharpness),
        [(t, 5 * t), (1, t), (8, t), (t, d), (t, d)],
        [place, pattern[0], s0, sa, sb, sc, sd, seam, queries, positive[None]],
        smem=2, later=[hop_q], flops=3 * one, name="softmax",
    )
    ta = send(term_a, swap_a)
    tb = send(term_b, swap_b)
    term_c, term_d = call(band_terms, [(t, d), (t, d)], [weights, queries], flops=2 * one, name="band_terms")
    tc = send(term_c, swap_c)
    td = send(term_d, swap_d)
    grad_queries, own = call(
        query_gradient,
        [(t, d), (t, d)],
        [place, weights, queries, keys, ka, kb, kc, kd, seam],
        smem=1, later=[term_c], flops=6 * one, name="query_gradient",
    )
    (aux,) = call(passed, [(8, t)], [aux], later=[grad_queries, ta], name="passed")
    aux_seam = send(aux, seam_swap())
    order = after(tb, aux_seam)
    order = after(tc, order)
    order = after(td, order)
    (some,) = call(key_sum, [(t, d)], [own, ta, tb, tc, td], later=[order], name="key_sum")
    (ss,) = call(functools.partial(seam_scores, sharpness), [(t, t)], [place, keys, seam_q], smem=1, later=[some], flops=one, name="seam_scores")
    (grad_keys,) = call(
        functools.partial(key_gradient, sharpness),
        [(t, d)],
        [place, some, ss, seam_q, aux_seam],
        smem=1, flops=one, name="key_gradient",
    )
    return loss[0], grad_queries, grad_keys


def solution(mesh):
    rows, flat = P(("loop", "group"), None), P(("loop", "group"))
    return jax.shard_map(
        local,
        mesh=mesh,
        in_specs=(rows, rows, rows, flat),
        out_specs=(flat, rows, rows),
        check_vma=False,
    )
```

```python
import functools
import math

import jax
import jax.numpy as jnp
from jax import lax
from jax.experimental import pallas as pl
from jax.experimental.pallas import tpu as pltpu
from jax.sharding import PartitionSpec as P

FULL = lax.Precision.HIGHEST
AXES = ("group", "loop")
BANDS, SECTORS, ZS = 64, 8, 8
SEAM = 31
FAR = 1e30
VMEM_BYTES = 24 * 1024 * 1024


def at(x, y, z, core):
    band = (y // 4) * 32 + x * ZS + z
    return band * SECTORS + (y % 4) * 2 + core


def seam_column(y, core, which):
    if (y % 4 >= 2) == (which == 1):
        return (3, 0) if core else (0, 7)
    if which == 0:
        return ((3, 0) if core else (1, 0)) if y < 4 else ((0, 0) if core else (2, 7))
    return (1 + core, 0) if y < 4 else (2 - core, 7)


def seam_pairs(which):
    out, onward = [], []
    for y in range(8):
        for core in range(2):
            up = y < 4
            here = at(3, y, 7, core) if up else at(0, y, 0, core)
            there = at(0, y + 4, 0, core) if up else at(3, y - 4, 7, core)
            x, z = seam_column(y, core, which)
            relay = at(x, y, z, core)
            out.append((here, relay))
            onward.append((relay, there))
    return out, onward


def sector_swap(first):
    pairs = []
    for b in range(BANDS):
        for s in range(first, SECTORS + first, 2):
            i, j = b * SECTORS + s, b * SECTORS + (s + 1) % SECTORS
            pairs += [(i, j), (j, i)]
    return pairs


def band_pairs(b):
    pairs = []
    for s in range(SECTORS):
        i, j = b * SECTORS + s, (b + 1) * SECTORS + s
        pairs += [(i, j), (j, i)]
    return pairs


def band_swap(first):
    return sum([band_pairs(b) for b in range(first, BANDS - 1, 2) if b != SEAM], [])


def seam_swap():
    return band_pairs(SEAM)


def send(value, pairs):
    return lax.ppermute(value, AXES, pairs)


def outer(a, b):
    return lax.dot_general(a, b, (((1,), (1,)), ((), ())), precision=FULL, preferred_element_type=jnp.float32)


def inner(a, b):
    return jnp.dot(a, b, precision=FULL, preferred_element_type=jnp.float32)


def call(body, out, args, smem=0, later=(), flops=0, name=None):
    vmem = pl.BlockSpec(memory_space=pltpu.VMEM)
    scalar = pl.BlockSpec(memory_space=pltpu.SMEM)
    out = [a if isinstance(a, jax.ShapeDtypeStruct) else jax.ShapeDtypeStruct(a, jnp.float32) for a in out]
    moved = sum(a.dtype.itemsize * math.prod(a.shape) for a in list(args) + out)
    count = len(args) - smem
    args = list(args) + list(later)

    def run(*refs):
        body(*refs[:smem + count], *refs[len(args):])

    return pl.pallas_call(
        run,
        out_shape=out,
        in_specs=[scalar] * smem + [vmem] * count + [pl.BlockSpec(memory_space=pl.ANY)] * len(later),
        out_specs=[vmem] * len(out),
        compiler_params=pltpu.CompilerParams(vmem_limit_bytes=VMEM_BYTES),
        cost_estimate=pl.CostEstimate(flops=flops, bytes_accessed=moved, transcendentals=0),
        name=name,
    )(*args)


def mark(out):
    out[...] = jnp.zeros_like(out)


def after(*arrays):
    return call(mark, [(8, 128)], [], later=arrays, name="after")[0]


def passed(value, out):
    out[...] = value[...]


def first_scores(sharpness, q, k, ka, s0, sa):
    big = q[...] * sharpness
    s0[...] = outer(big, k[...])
    sa[...] = outer(big, ka[...])


def scores(sharpness, q, k, s):
    s[...] = outer(q[...] * sharpness, k[...])


def scores_and_copy(sharpness, q, k, s, sent):
    s[...] = outer(q[...] * sharpness, k[...])
    sent[...] = q[...]


def column(row):
    return jnp.broadcast_to(row, (128, row.shape[1])).T[:, :1]


def as_row(col):
    return jnp.broadcast_to(col, (col.shape[0], 128)).T[:1]


def softmax(sharpness, place, allowed, s0, sa, sb, sc, sd, seam, q, positive, weights, loss, aux, term_a, term_b):
    t = q.shape[0]
    for o, s in enumerate((s0, sa, sb, sc, sd)):
        weights[:, o * t:(o + 1) * t] = s[...]

    @pl.when(place[0] > 0)
    def _():
        weights[:, 4 * t:] = outer(q[...] * sharpness, seam[...])

    pick = column(positive[...])
    columns = lax.broadcasted_iota(jnp.int32, (t, t), 1)
    blocks = [weights[:, o * t:(o + 1) * t] for o in range(5)]
    masked = [jnp.where(allowed[place[1 + o]] > 0, b, -FAR) for o, b in enumerate(blocks)]
    highest = jnp.max(functools.reduce(jnp.maximum, masked), axis=1, keepdims=True)
    powers = [jnp.exp(m - highest) for m in masked]
    total = jnp.sum(sum(powers), axis=1, keepdims=True)
    log_total = highest + jnp.log(total)
    hits = [pick == columns + place[1 + o] * t for o in range(5)]
    score = sum(jnp.where(h, b, 0.0) for h, b in zip(hits, blocks))
    loss[...] = as_row(log_total - jnp.sum(score, axis=1, keepdims=True))
    share = sharpness / total
    for o, (p, h) in enumerate(zip(powers, hits)):
        weights[:, o * t:(o + 1) * t] = p * share - jnp.where(h, sharpness, 0.0)
    logs = as_row(log_total)
    aux[...] = jnp.zeros_like(aux)
    for o in range(5):
        aux[o:o + 1] = jnp.where(allowed[o] > 0, logs, FAR)
    aux[5:6] = positive[...].astype(jnp.float32)
    term_b[...] = inner(weights[:, 2 * t:3 * t].T, q[...])
    term_a[...] = inner(weights[:, t:2 * t].T, q[...])


def query_gradient(place, weights, q, k, ka, kb, kc, kd, seam, gq, own):
    t = k.shape[0]
    own[...] = inner(weights[:, :t].T, q[...])
    weight = lambda o: weights[:, o * t:(o + 1) * t]
    total = inner(weight(0), k[...])
    for o, key in enumerate((ka, kb, kc)):
        total += inner(weight(o + 1), key[...])
    gq[...] = total

    @pl.when(place[0] > 0)
    def _():
        gq[...] += inner(weight(4), seam[...])

    @pl.when(place[0] == 0)
    def _():
        gq[...] += inner(weight(4), kd[...])


def seam_or(sharpness, place, k, q, seam, s):
    @pl.when(place[0] > 0)
    def _():
        s[...] = outer(k[...] * sharpness, seam[...])

    @pl.when(place[0] == 0)
    def _():
        s[...] = outer(k[...] * sharpness, q[...])


def key_weights(sharpness, slot, s, aux):
    t = s.shape[0]
    back = jnp.where(slot % 2 == 1, slot + 1, slot - 1)
    logs = aux[1:2]
    for o in range(2, 5):
        logs = jnp.where(back == o, aux[o:o + 1], logs)
    rows = lax.broadcasted_iota(jnp.int32, (t, t), 0) + back * t
    hits = rows == aux[5:6].astype(jnp.int32)
    return (jnp.exp(s[...] - logs) - jnp.where(hits, 1.0, 0.0)) * sharpness


def keys_c(sharpness, place, own, ta, tc, qc, aux, out):
    total = own[...] + ta[...]
    out[...] = total + inner(key_weights(sharpness, place[4], tc, aux), qc[...])


def keys_d(sharpness, place, some, td, qd, seam, aux, out):
    w = key_weights(sharpness, place[5], td, aux)

    @pl.when(place[0] > 0)
    def _():
        out[...] = some[...] + inner(w, seam[...])

    @pl.when(place[0] == 0)
    def _():
        out[...] = some[...] + inner(w, qd[...])


def key_sum(some, tb, out):
    out[...] = some[...] + tb[...]


def local(queries, keys, pattern, positive):
    t, d = queries.shape
    sharpness = math.sqrt(d)
    one = 2 * t * t * d
    band, sector = lax.axis_index("group"), lax.axis_index("loop")
    odd_band, odd_sector = band % 2, sector % 2
    at_seam = (band == SEAM) | (band == SEAM + 1)
    place = jnp.stack([
        at_seam.astype(jnp.int32),
        0 * band,
        2 - odd_sector,
        1 + odd_sector,
        4 - odd_band,
        3 + odd_band,
    ])
    swap_a, swap_b = sector_swap(0), sector_swap(1)
    swap_c, swap_d = band_swap(0), band_swap(1)
    out_k, onward_k = seam_pairs(0)
    out_q, onward_q = seam_pairs(1)
    score = functools.partial(call, functools.partial(scores, sharpness), [(t, t)], flops=one)

    hop = send(keys, out_k)
    kb = send(keys, swap_b)
    kc = send(keys, swap_c)
    kd = send(keys, swap_d)
    ka = send(keys, swap_a)
    s0, sa = call(
        functools.partial(first_scores, sharpness),
        [(t, t), (t, t)],
        [queries, keys, ka], later=[hop], flops=2 * one, name="first_scores",
    )
    seam = send(hop, onward_k)
    hop_q = send(queries, out_q)
    sb, sent = call(
        functools.partial(scores_and_copy, sharpness), [(t, t), (t, d)],
        [queries, kb], later=[s0], flops=one, name="scores_b",
    )
    qc = send(sent, swap_c)
    qd = send(sent, swap_d)
    (sc,) = score([queries, kc], later=[sb], name="scores_c")
    (sd,) = score([queries, kd], later=[sc], name="scores_d")
    seam_q = send(hop_q, onward_q)
    weights, loss, aux, term_a, term_b = call(
        functools.partial(softmax, sharpness),
        [(t, 5 * t), (1, t), (8, t), (t, d), (t, d)],
        [place, pattern[0], s0, sa, sb, sc, sd, seam, queries, positive[None]],
        smem=2, later=[hop_q], flops=3 * one, name="softmax",
    )
    grad_queries, own = call(
        query_gradient,
        [(t, d), (t, d)],
        [place, weights, queries, keys, ka, kb, kc, kd, seam],
        smem=1, flops=6 * one, name="query_gradient",
    )
    (tc,) = score([keys, qc], later=[own], name="back_c")
    tb = send(term_b, swap_b)
    ta = send(term_a, swap_a)
    aux_c = send(aux, swap_c)
    aux_d = send(aux, swap_d + seam_swap())
    (td,) = call(
        functools.partial(seam_or, sharpness), [(t, t)],
        [place, keys, qd, seam_q], smem=1, later=[tc], flops=one, name="back_d",
    )
    (some,) = call(
        functools.partial(keys_c, sharpness), [(t, d)],
        [place, own, ta, tc, qc, aux_c], smem=1, later=[td], flops=one, name="keys_c",
    )
    (some,) = call(
        functools.partial(keys_d, sharpness), [(t, d)],
        [place, some, td, qd, seam_q, aux_d], smem=1, flops=one, name="keys_d",
    )
    (grad_keys,) = call(key_sum, [(t, d)], [some, tb], name="key_sum")
    return loss[0], grad_queries, grad_keys


def solution(mesh):
    rows, flat = P(("loop", "group"), None), P(("loop", "group"))
    return jax.shard_map(
        local,
        mesh=mesh,
        in_specs=(rows, rows, rows, flat),
        out_specs=(flat, rows, rows),
        check_vma=False,
    )
```

```python
import functools
import math

import jax
import jax.numpy as jnp
from jax import lax
from jax.experimental import pallas as pl
from jax.experimental.pallas import tpu as pltpu
from jax.sharding import PartitionSpec as P

FULL = lax.Precision.HIGHEST
AXES = ("group", "loop")
BANDS, SECTORS, ZS = 64, 8, 8
SEAM = 31
FAR = 1e30
VMEM_BYTES = 24 * 1024 * 1024


def at(x, y, z, core):
    band = (y // 4) * 32 + x * ZS + z
    return band * SECTORS + (y % 4) * 2 + core


def seam_column(y, core, which):
    if (y % 4 >= 2) == (which == 1):
        return (3, 0) if core else (0, 7)
    if which == 0:
        return ((3, 0) if core else (1, 0)) if y < 4 else ((0, 0) if core else (2, 7))
    return (1 + core, 0) if y < 4 else (2 - core, 7)


def seam_pairs(which):
    out, onward = [], []
    for y in range(8):
        for core in range(2):
            up = y < 4
            here = at(3, y, 7, core) if up else at(0, y, 0, core)
            there = at(0, y + 4, 0, core) if up else at(3, y - 4, 7, core)
            x, z = seam_column(y, core, which)
            relay = at(x, y, z, core)
            out.append((here, relay))
            onward.append((relay, there))
    return out, onward


def sector_swap(first):
    pairs = []
    for b in range(BANDS):
        for s in range(first, SECTORS + first, 2):
            i, j = b * SECTORS + s, b * SECTORS + (s + 1) % SECTORS
            pairs += [(i, j), (j, i)]
    return pairs


def band_pairs(b):
    pairs = []
    for s in range(SECTORS):
        i, j = b * SECTORS + s, (b + 1) * SECTORS + s
        pairs += [(i, j), (j, i)]
    return pairs


def band_swap(first):
    return sum([band_pairs(b) for b in range(first, BANDS - 1, 2) if b != SEAM], [])


def seam_swap():
    return band_pairs(SEAM)


def send(value, pairs):
    return lax.ppermute(value, AXES, pairs)


def outer(a, b):
    return lax.dot_general(a, b, (((1,), (1,)), ((), ())), precision=FULL, preferred_element_type=jnp.float32)


def inner(a, b):
    return jnp.dot(a, b, precision=FULL, preferred_element_type=jnp.float32)


def call(body, out, args, smem=0, later=(), flops=0, name=None):
    vmem = pl.BlockSpec(memory_space=pltpu.VMEM)
    scalar = pl.BlockSpec(memory_space=pltpu.SMEM)
    out = [a if isinstance(a, jax.ShapeDtypeStruct) else jax.ShapeDtypeStruct(a, jnp.float32) for a in out]
    moved = sum(a.dtype.itemsize * math.prod(a.shape) for a in list(args) + out)
    count = len(args) - smem
    args = list(args) + list(later)

    def run(*refs):
        body(*refs[:smem + count], *refs[len(args):])

    return pl.pallas_call(
        run,
        out_shape=out,
        in_specs=[scalar] * smem + [vmem] * count + [pl.BlockSpec(memory_space=pl.ANY)] * len(later),
        out_specs=[vmem] * len(out),
        compiler_params=pltpu.CompilerParams(vmem_limit_bytes=VMEM_BYTES),
        cost_estimate=pl.CostEstimate(flops=flops, bytes_accessed=moved, transcendentals=0),
        name=name,
    )(*args)


def mark(out):
    out[...] = jnp.zeros_like(out)


def after(*arrays):
    return call(mark, [(8, 128)], [], later=arrays, name="after")[0]


def passed(value, out):
    out[...] = value[...]


def first_scores(sharpness, q, k, ka, s0, sa):
    big = q[...] * sharpness
    s0[...] = outer(big, k[...])
    sa[...] = outer(big, ka[...])


def scores(sharpness, q, k, s):
    s[...] = outer(q[...] * sharpness, k[...])


def scores_and_copy(sharpness, q, k, s, sent):
    s[...] = outer(q[...] * sharpness, k[...])
    sent[...] = q[...]


def column(row):
    return jnp.broadcast_to(row, (128, row.shape[1])).T[:, :1]


def as_row(col):
    return jnp.broadcast_to(col, (col.shape[0], 128)).T[:1]


def softmax(sharpness, place, allowed, s0, sa, sb, sc, sd, seam, q, positive, weights, loss, aux, term_a, term_b):
    t = q.shape[0]
    for o, s in enumerate((s0, sa, sb, sc, sd)):
        weights[:, o * t:(o + 1) * t] = s[...]

    @pl.when(place[0] > 0)
    def _():
        weights[:, 4 * t:] = outer(q[...] * sharpness, seam[...])

    pick = column(positive[...])
    columns = lax.broadcasted_iota(jnp.int32, (t, t), 1)
    blocks = [weights[:, o * t:(o + 1) * t] for o in range(5)]
    masked = [jnp.where(allowed[place[1 + o]] > 0, b, -FAR) for o, b in enumerate(blocks)]
    highest = jnp.max(functools.reduce(jnp.maximum, masked), axis=1, keepdims=True)
    powers = [jnp.exp(m - highest) for m in masked]
    total = jnp.sum(sum(powers), axis=1, keepdims=True)
    log_total = highest + jnp.log(total)
    hits = [pick == columns + place[1 + o] * t for o in range(5)]
    score = sum(jnp.where(h, b, 0.0) for h, b in zip(hits, blocks))
    loss[...] = as_row(log_total - jnp.sum(score, axis=1, keepdims=True))
    share = sharpness / total
    for o, (p, h) in enumerate(zip(powers, hits)):
        weights[:, o * t:(o + 1) * t] = p * share - jnp.where(h, sharpness, 0.0)
    logs = as_row(log_total)
    aux[...] = jnp.zeros_like(aux)
    for o in range(5):
        aux[o:o + 1] = jnp.where(allowed[o] > 0, logs, FAR)
    aux[5:6] = positive[...].astype(jnp.float32)
    term_b[...] = inner(weights[:, 2 * t:3 * t].T, q[...])
    term_a[...] = inner(weights[:, t:2 * t].T, q[...])


def query_gradient(place, weights, q, k, ka, kb, kc, kd, seam, gq, own):
    t = k.shape[0]
    own[...] = inner(weights[:, :t].T, q[...])
    weight = lambda o: weights[:, o * t:(o + 1) * t]
    total = inner(weight(0), k[...])
    for o, key in enumerate((ka, kb, kc)):
        total += inner(weight(o + 1), key[...])
    gq[...] = total

    @pl.when(place[0] > 0)
    def _():
        gq[...] += inner(weight(4), seam[...])

    @pl.when(place[0] == 0)
    def _():
        gq[...] += inner(weight(4), kd[...])


def seam_or(sharpness, place, k, q, seam, s):
    @pl.when(place[0] > 0)
    def _():
        s[...] = outer(k[...] * sharpness, seam[...])

    @pl.when(place[0] == 0)
    def _():
        s[...] = outer(k[...] * sharpness, q[...])


def key_weights(sharpness, slot, s, aux):
    t = s.shape[0]
    back = jnp.where(slot % 2 == 1, slot + 1, slot - 1)
    logs = aux[1:2]
    for o in range(2, 5):
        logs = jnp.where(back == o, aux[o:o + 1], logs)
    rows = lax.broadcasted_iota(jnp.int32, (t, t), 0) + back * t
    hits = rows == aux[5:6].astype(jnp.int32)
    return (jnp.exp(s[...] - logs) - jnp.where(hits, 1.0, 0.0)) * sharpness


def keys_c(sharpness, place, own, ta, tc, qc, aux, out):
    total = own[...] + ta[...]
    out[...] = total + inner(key_weights(sharpness, place[4], tc, aux), qc[...])


def keys_d(sharpness, place, some, td, qd, seam, aux, out):
    w = key_weights(sharpness, place[5], td, aux)

    @pl.when(place[0] > 0)
    def _():
        out[...] = some[...] + inner(w, seam[...])

    @pl.when(place[0] == 0)
    def _():
        out[...] = some[...] + inner(w, qd[...])


def key_sum(some, tb, out):
    out[...] = some[...] + tb[...]


def local(queries, keys, pattern, positive):
    t, d = queries.shape
    sharpness = math.sqrt(d)
    one = 2 * t * t * d
    band, sector = lax.axis_index("group"), lax.axis_index("loop")
    odd_band, odd_sector = band % 2, sector % 2
    at_seam = (band == SEAM) | (band == SEAM + 1)
    place = jnp.stack([
        at_seam.astype(jnp.int32),
        0 * band,
        2 - odd_sector,
        1 + odd_sector,
        4 - odd_band,
        3 + odd_band,
    ])
    swap_a, swap_b = sector_swap(0), sector_swap(1)
    swap_c, swap_d = band_swap(0), band_swap(1)
    out_k, onward_k = seam_pairs(0)
    out_q, onward_q = seam_pairs(1)
    score = functools.partial(call, functools.partial(scores, sharpness), [(t, t)], flops=one)

    hop = send(keys, out_k)
    kb = send(keys, swap_b)
    kc = send(keys, swap_c)
    kd = send(keys, swap_d)
    ka = send(keys, swap_a)
    s0, sa = call(
        functools.partial(first_scores, sharpness),
        [(t, t), (t, t)],
        [queries, keys, ka], later=[hop], flops=2 * one, name="first_scores",
    )
    seam = send(hop, onward_k)
    hop_q = send(queries, out_q)
    sb, sent = call(
        functools.partial(scores_and_copy, sharpness), [(t, t), (t, d)],
        [queries, kb], later=[s0], flops=one, name="scores_b",
    )
    qc = send(sent, swap_c)
    qd = send(sent, swap_d)
    (sc,) = score([queries, kc], later=[sb], name="scores_c")
    (sd,) = score([queries, kd], later=[sc], name="scores_d")
    seam_q = send(hop_q, onward_q)
    weights, loss, aux, term_a, term_b = call(
        functools.partial(softmax, sharpness),
        [(t, 5 * t), (1, t), (8, t), (t, d), (t, d)],
        [place, pattern[0], s0, sa, sb, sc, sd, seam, queries, positive[None]],
        smem=2, later=[hop_q], flops=3 * one, name="softmax",
    )
    (tc,) = score([keys, qc], later=[weights], name="back_c")
    tb = send(term_b, swap_b)
    ta = send(term_a, swap_a)
    aux_c = send(aux, swap_c)
    aux_d = send(aux, swap_d + seam_swap())
    grad_queries, own = call(
        query_gradient,
        [(t, d), (t, d)],
        [place, weights, queries, keys, ka, kb, kc, kd, seam],
        smem=1, later=[tc], flops=6 * one, name="query_gradient",
    )
    (td,) = call(
        functools.partial(seam_or, sharpness), [(t, t)],
        [place, keys, qd, seam_q], smem=1, later=[own], flops=one, name="back_d",
    )
    (some,) = call(
        functools.partial(keys_c, sharpness), [(t, d)],
        [place, own, ta, tc, qc, aux_c], smem=1, later=[td], flops=one, name="keys_c",
    )
    (some,) = call(
        functools.partial(keys_d, sharpness), [(t, d)],
        [place, some, td, qd, seam_q, aux_d], smem=1, flops=one, name="keys_d",
    )
    (grad_keys,) = call(key_sum, [(t, d)], [some, tb], name="key_sum")
    return loss[0], grad_queries, grad_keys


def solution(mesh):
    rows, flat = P(("loop", "group"), None), P(("loop", "group"))
    return jax.shard_map(
        local,
        mesh=mesh,
        in_specs=(rows, rows, rows, flat),
        out_specs=(flat, rows, rows),
        check_vma=False,
    )
```
